32 devices in a mesh: dp: 4 (over y, core), expert: 8 (over z, x).
Axes of the slice: x: 2, y: 2, z: 4, core: 2. Of those that a mesh axis runs over, the one named last changes fastest.
Arguments:
- tokens: bfloat16 [4096, 2048], P(('dp', 'expert')), may hold values from -6 to 6
- expert_ids: int32 [4096, 2], P(('dp', 'expert')), may hold values from 0 to 7, all different within a row; in each aligned block of 128 rows (0 to 127, 128 to 255, ...) at most 48 rows name the same one
- gate_values: float32 [4096, 2], P(('dp', 'expert')), may hold values from 0.1 to 1
- cotangent: bfloat16 [4096, 2048], P(('dp', 'expert')), may hold values from -5 to 5
- w_gate: bfloat16 [8, 2048, 704], P('expert', None, 'dp'), may hold values from -0.125 to 0.125
- w_up: bfloat16 [8, 2048, 704], P('expert', None, 'dp'), may hold values from -0.125 to 0.125
- w_down: bfloat16 [8, 704, 2048], P('expert', 'dp'), may hold values from -0.21875 to 0.21875
Outputs:
- mixed: bfloat16 [4096, 2048], P(('dp', 'expert'))
- grad_tokens: bfloat16 [4096, 2048], P(('dp', 'expert'))
- grad_gate: bfloat16 [8, 2048, 704], P('expert', None, 'dp')
- grad_up: bfloat16 [8, 2048, 704], P('expert', None, 'dp')
- grad_down: bfloat16 [8, 704, 2048], P('expert', 'dp')
The draws below stay inside these ranges and needn't reach their ends.
Inputs may be any that keep to these rules, and one draw needn't show every extreme that they name: `expert_ids`: each row names 2 different experts. Among the 128 rows of one device no expert is named more than 48 times, and in the rows of some devices an expert is named exactly 48 times.
All inputs are finite; a program needn't handle non-finite values.
Results may differ from the reference program's by a relative error of at most 0.0065.
Values may be sent and summed in bfloat16 or wider, within the bound.
A program may use at most 128 MiB of HBM per device.

```python
import math
import jax
import jax.numpy as jnp
import numpy as np
from jax import lax

D = 2048
FF = 704
TOP = 2
TOK_DEV = 128
EXPERTS = 8
CAP = 48
TOKENS = 4096
N_DP = 4
N_EXPERT = 8


def block_levels(rng, dims, cuts, smallest, largest):
    factor_of = 1.0
    for axis_at, blocks in cuts:
        draws = jax.random.uniform(jax.random.fold_in(jax.random.fold_in(rng, 6), axis_at), (blocks,), jnp.float32, smallest / len(cuts), largest / len(cuts))
        factor_of = factor_of * jnp.repeat(jnp.exp(draws), dims[axis_at] // blocks).reshape((-1,) + (1,) * (len(dims) - 1 - axis_at))
    return factor_of


def shared_out(key, own, number, rows, number_of, top, most, slope):
    sequence = jax.random.permutation(key, number_of)
    crowded, common = shares(number_of, rows * top, most, slope, True), shares(number_of, rows * top, most, slope, False)
    places = jnp.arange(number_of)

    def named(sizes, turn):
        used = int((sizes > 0).sum())
        fixed = max(1, used // 4)
        shifted = fixed + (places - fixed + turn * (used - fixed)) % max(1, number_of - fixed)
        return jnp.zeros((number_of,), jnp.int32).at[sequence[jnp.where(places < fixed, places, shifted)]].set(jnp.asarray(sizes, jnp.int32))

    sizes = jnp.where(number % 4 == 0, named(crowded, number // 4), named(common, number - number // 4 - 1))
    mixed = jax.random.permutation(jax.random.fold_in(own, 3), number_of)
    giver, receiver = mixed[0:number_of // 2 * 2:2], mixed[1:number_of // 2 * 2:2]
    room = jnp.minimum(sizes[giver] - 1, most - sizes[receiver]) // 2
    room = jnp.where((giver == sequence[0]) | (receiver == sequence[0]) | (sizes[receiver] == 0), 0, jnp.maximum(room, 0))
    shifted = jax.random.randint(jax.random.fold_in(own, 4), (number_of // 2,), 0, 1 << 20) % (room + 1)
    sizes = sizes.at[giver].add(-shifted).at[receiver].add(shifted)
    items = jnp.searchsorted(jnp.cumsum(sizes), jnp.arange(rows * top), side="right").astype(jnp.int32)
    grid = items.reshape(top, rows).T
    grid = grid[jax.random.permutation(jax.random.fold_in(own, 1), rows)]
    turn = jax.random.randint(jax.random.fold_in(own, 2), (rows, 1), 0, top)
    return jnp.take_along_axis(grid, (jnp.arange(top)[None, :] + turn) % top, axis=1)


def shares(number_of, total, limit, skew, full):
    weights = [(1 << 20) // math.isqrt(grade ** skew) + 1 for grade in range(1, number_of + 1)]
    largest = limit if full else min(limit, max(-(-total // number_of), total * weights[0] // sum(weights)))
    least = 1 if total - largest >= number_of - 1 else 0
    given, rest = [largest] + [least] * (number_of - 1), total - largest - least * (number_of - 1)
    while rest > 0:
        candidates = [i for i in range(1, number_of) if given[i] < largest] or [i for i in range(1, number_of) if given[i] < limit]
        mass, budget = sum([weights[i] for i in candidates]), rest
        for i in candidates:
            more = min(limit - given[i], max(1, budget * weights[i] // mass), rest)
            given[i] = given[i] + more
            rest = rest - more
    return np.array(given)


def noise(key, extent, spread, most, split=(), held_as=jnp.bfloat16):
    loudness = block_levels(key, extent, split, -0.22, 0.18) if split else 1.0
    values = jax.random.normal(key, extent, jnp.float32) * spread * loudness
    return jnp.minimum(jnp.maximum(values, -most), most).astype(held_as)


def setup_inputs(seed: int = 0) -> dict:
    arg_keys = jax.random.split(jax.random.key(seed), 8)
    tokens = noise(arg_keys[0], (TOKENS, D), 1.0, 6.0, ((0, 32),))
    expert_ids_keys = jax.random.split(jax.random.fold_in(arg_keys[1], 1), TOKENS // TOK_DEV)
    expert_ids_turns = jax.random.permutation(jax.random.fold_in(arg_keys[1], 3), TOKENS // TOK_DEV)
    expert_ids = jax.vmap(lambda own, number: shared_out(jax.random.fold_in(arg_keys[1], 2), own, number, TOK_DEV, EXPERTS, TOP, CAP, 2))(expert_ids_keys, expert_ids_turns).reshape((TOKENS, TOP))
    gate_values = jnp.clip(jnp.exp(math.log(1.0) - 2.3025851 * jax.random.uniform(arg_keys[2], (TOKENS, TOP), jnp.float32) ** block_levels(arg_keys[2], (TOKENS, TOP), ((0, 32),), -0.2, 0.2)), 0.1, 1.0)
    cotangent = noise(arg_keys[3], (TOKENS, D), 0.35, 5.0, ((0, 32),))
    w_gate = noise(arg_keys[4], (EXPERTS, D, FF), D ** -0.5, 0.125, ((0, 8), (2, 4)))
    w_up = noise(arg_keys[5], (EXPERTS, D, FF), D ** -0.5, 0.125, ((0, 8), (2, 4)))
    w_down = noise(arg_keys[6], (EXPERTS, FF, D), FF ** -0.5, 0.21875, ((0, 8), (1, 4)))
    return dict(tokens=tokens, expert_ids=expert_ids, gate_values=gate_values, cotangent=cotangent, w_gate=w_gate, w_up=w_up, w_down=w_down)


def swiglu_parts(gate_pre):
    sigmoid_g = jax.nn.sigmoid(gate_pre)
    return gate_pre * sigmoid_g, sigmoid_g * (1.0 + gate_pre * (1.0 - sigmoid_g))


def contract_rows(left, right):
    return lax.dot_general(left, right, (((0,), (0,)), ((), ())), preferred_element_type=jnp.float32)


def contract_cols(left, right):
    return lax.dot_general(left, right, (((1,), (1,)), ((), ())), preferred_element_type=jnp.float32)


def expert_pass(slot_rows, slot_grads, weight_gate, weight_up, weight_down):
    gate_pre = jnp.dot(slot_rows, weight_gate, preferred_element_type=jnp.float32)
    up_pre = jnp.dot(slot_rows, weight_up, preferred_element_type=jnp.float32)
    activated, act_slope = swiglu_parts(gate_pre)
    hidden = (activated * up_pre).astype(jnp.bfloat16)
    expert_out = jnp.dot(hidden, weight_down, preferred_element_type=jnp.float32)
    grad_hidden = contract_cols(slot_grads, weight_down)
    grad_gate_pre = (grad_hidden * up_pre * act_slope).astype(jnp.bfloat16)
    grad_up_pre = (grad_hidden * activated).astype(jnp.bfloat16)
    grad_row = contract_cols(grad_gate_pre, weight_gate) + contract_cols(grad_up_pre, weight_up)
    return expert_out, grad_row, grad_gate_pre, grad_up_pre, hidden


def reference(tokens, expert_ids, gate_values, cotangent, w_gate, w_up, w_down):
    flat_ids = expert_ids.reshape(-1).astype(jnp.int32)
    assign_total = flat_ids.shape[0]
    sorted_idx = jnp.argsort(flat_ids, stable=True).astype(jnp.int32)
    counts = jnp.sum((flat_ids[:, None] == jnp.arange(EXPERTS, dtype=jnp.int32)[None, :]).astype(jnp.int32), axis=0)
    starts = (jnp.cumsum(counts) - counts).astype(jnp.int32)
    most_rows = N_DP * N_EXPERT * CAP
    flat_gates = gate_values.reshape(-1)

    def one_expert(expert):
        position = jnp.arange(most_rows, dtype=jnp.int32)
        is_valid = position < counts[expert]
        assign_idx = sorted_idx[jnp.minimum(starts[expert] + position, assign_total - 1).astype(jnp.int32)]
        token_idx = (assign_idx // TOP).astype(jnp.int32)
        weights = jnp.where(is_valid, flat_gates[assign_idx], jnp.zeros_like(flat_gates[assign_idx]))
        slot_rows = tokens[token_idx]
        slot_grads = (weights[:, None] * cotangent[token_idx].astype(jnp.float32)).astype(jnp.bfloat16)
        expert_out, grad_row, grad_gate_pre, grad_up_pre, hidden = expert_pass(
            slot_rows, slot_grads, w_gate[expert], w_up[expert], w_down[expert])
        grad_gate = contract_rows(slot_rows, grad_gate_pre).astype(jnp.bfloat16)
        grad_up = contract_rows(slot_rows, grad_up_pre).astype(jnp.bfloat16)
        grad_down = contract_rows(hidden, slot_grads).astype(jnp.bfloat16)
        target = jnp.where(is_valid, assign_idx, assign_total).astype(jnp.int32)
        return expert_out.astype(jnp.bfloat16), grad_row.astype(jnp.bfloat16), target, grad_gate, grad_up, grad_down

    per_expert = lax.map(one_expert, jnp.arange(EXPERTS, dtype=jnp.int32))
    expert_out, grad_rows, targets, grad_gate, grad_up, grad_down = per_expert
    flat_targets = targets.reshape(-1)
    placed_out = jnp.zeros((assign_total + 1, D), jnp.bfloat16).at[flat_targets].set(expert_out.reshape(-1, D))[:assign_total]
    placed_grad = jnp.zeros((assign_total + 1, D), jnp.bfloat16).at[flat_targets].set(grad_rows.reshape(-1, D))[:assign_total]
    mixed = jnp.sum(placed_out.reshape(-1, TOP, D).astype(jnp.float32) * gate_values[:, :, None], axis=1).astype(jnp.bfloat16)
    grad_tokens = jnp.sum(placed_grad.reshape(-1, TOP, D).astype(jnp.float32), axis=1).astype(jnp.bfloat16)
    return mixed, grad_tokens, grad_gate, grad_up, grad_down
```

```python
import jax
import jax.numpy as jnp
from jax import lax
from jax.sharding import PartitionSpec as P


def swiglu_parts(gate_pre):
    sigmoid_g = jax.nn.sigmoid(gate_pre)
    return (gate_pre * sigmoid_g, sigmoid_g * (1.0 + gate_pre * (1.0 - sigmoid_g)))


def contract_rows(left, right):
    return lax.dot_general(
        left, right, (((0,), (0,)), ((), ())), preferred_element_type=jnp.float32
    )


def contract_cols(left, right):
    return lax.dot_general(
        left, right, (((1,), (1,)), ((), ())), preferred_element_type=jnp.float32
    )


def body(tokens, expert_ids, gate_values, cotangent, w_gate, w_up, w_down):
    token_count, feature = tokens.shape
    routes_per = expert_ids.shape[1]
    experts = lax.axis_size("expert")
    capacity = 3 * token_count * routes_per // (2 * experts)
    slot_count = experts * capacity
    route_count = token_count * routes_per
    flat_ids = expert_ids.reshape(-1)
    one_hot = flat_ids[:, None] == jnp.arange(experts, dtype=jnp.int32)[None, :]
    order = jnp.arange(route_count, dtype=jnp.int32)
    earlier = (order[None, :] < order[:, None]).astype(jnp.bfloat16)
    before = jnp.dot(earlier, one_hot.astype(jnp.bfloat16), preferred_element_type=jnp.float32)
    slot_rank = jnp.sum(jnp.where(one_hot, before, 0.0), axis=1).astype(jnp.int32)
    slot_of = (flat_ids * capacity + slot_rank).reshape(token_count, routes_per)
    slots = jnp.arange(slot_count, dtype=jnp.int32)
    token_pick = jnp.zeros((slot_count, token_count), jnp.bool_)
    slot_gate = jnp.zeros((slot_count,), jnp.float32)
    mix = jnp.zeros((token_count, slot_count), jnp.float32)
    spread = jnp.zeros((token_count, slot_count), jnp.bool_)
    for route in range(routes_per):
        chosen = slots[:, None] == slot_of[None, :, route]
        token_pick = token_pick | chosen
        slot_gate = slot_gate + jnp.sum(jnp.where(chosen, gate_values[None, :, route], 0.0), axis=1)
        chosen = slot_of[:, route, None] == slots[None, :]
        spread = spread | chosen
        mix = mix + jnp.where(chosen, gate_values[:, route, None], 0.0)
    token_pick = token_pick.astype(jnp.bfloat16)
    spread = spread.astype(jnp.bfloat16)
    mix_high = mix.astype(jnp.bfloat16)
    mix_low = (mix - mix_high.astype(jnp.float32)).astype(jnp.bfloat16)
    shaped = (experts, capacity, feature)

    def exchange(rows):
        return lax.all_to_all(
            rows.reshape(shaped), "expert", split_axis=0, concat_axis=0, tiled=True
        ).reshape(slot_count, feature)

    send_rows = jnp.dot(token_pick, tokens, preferred_element_type=jnp.float32).astype(jnp.bfloat16)
    slot_rows = exchange(send_rows)
    send_grads = (
        slot_gate[:, None] * jnp.dot(token_pick, cotangent, preferred_element_type=jnp.float32)
    ).astype(jnp.bfloat16)
    slot_grads = exchange(send_grads)
    full_gate, full_up, full_down = (
        lax.all_gather(w_gate[0], "dp", axis=1, tiled=True),
        lax.all_gather(w_up[0], "dp", axis=1, tiled=True),
        lax.all_gather(w_down[0], "dp", axis=0, tiled=True),
    )
    gate_pre = jnp.dot(slot_rows, full_gate, preferred_element_type=jnp.float32)
    up_pre = jnp.dot(slot_rows, full_up, preferred_element_type=jnp.float32)
    activated, act_slope = swiglu_parts(gate_pre)
    hidden = (activated * up_pre).astype(jnp.bfloat16)
    out_rows = jnp.dot(hidden, full_down, preferred_element_type=jnp.float32).astype(jnp.bfloat16)
    out_rows, slot_grads = lax.optimization_barrier((out_rows, slot_grads))
    back_out = exchange(out_rows)
    grad_hidden = contract_cols(slot_grads, full_down)
    grad_gate_pre = (grad_hidden * up_pre * act_slope).astype(jnp.bfloat16)
    grad_up_pre = (grad_hidden * activated).astype(jnp.bfloat16)
    grad_rows = (
        contract_cols(grad_gate_pre, full_gate) + contract_cols(grad_up_pre, full_up)
    ).astype(jnp.bfloat16)
    back_grad = exchange(grad_rows)
    sum_gate, sum_up, sum_down = (
        lax.psum_scatter(
            contract_rows(left, right).astype(jnp.bfloat16), "dp", scatter_dimension=0, tiled=True
        )
        for left, right in (
            (grad_gate_pre, slot_rows),
            (grad_up_pre, slot_rows),
            (hidden, slot_grads),
        )
    )
    grad_gate = sum_gate.T[None]
    grad_up = sum_up.T[None]
    grad_down = sum_down[None]
    mixed = (
        jnp.dot(mix_high, back_out, preferred_element_type=jnp.float32)
        + jnp.dot(mix_low, back_out, preferred_element_type=jnp.float32)
    ).astype(jnp.bfloat16)
    grad_tokens = jnp.dot(spread, back_grad, preferred_element_type=jnp.float32).astype(
        jnp.bfloat16
    )
    return (mixed, grad_tokens, grad_gate, grad_up, grad_down)


def solution(mesh):
    in_specs = (
        P(("dp", "expert"), None),
        P(("dp", "expert"), None),
        P(("dp", "expert"), None),
        P(("dp", "expert"), None),
        P("expert", None, "dp"),
        P("expert", None, "dp"),
        P("expert", "dp", None),
    )
    out_specs = (
        P(("dp", "expert"), None),
        P(("dp", "expert"), None),
        P("expert", None, "dp"),
        P("expert", None, "dp"),
        P("expert", "dp", None),
    )
    return jax.shard_map(body, mesh=mesh, in_specs=in_specs, out_specs=out_specs, check_vma=False)
```

```python
import jax
import jax.numpy as jnp
from jax import lax
from jax.sharding import PartitionSpec as P


def swiglu_parts(gate_pre):
    sigmoid_g = jax.nn.sigmoid(gate_pre)
    return (gate_pre * sigmoid_g, sigmoid_g * (1.0 + gate_pre * (1.0 - sigmoid_g)))


def contract_rows(left, right):
    return lax.dot_general(
        left, right, (((0,), (0,)), ((), ())), preferred_element_type=jnp.float32
    )


def contract_cols(left, right):
    return lax.dot_general(
        left, right, (((1,), (1,)), ((), ())), preferred_element_type=jnp.float32
    )


def body(tokens, expert_ids, gate_values, cotangent, w_gate, w_up, w_down):
    token_count, feature = tokens.shape
    routes_per = expert_ids.shape[1]
    experts = lax.axis_size("expert")
    capacity = 3 * token_count * routes_per // (2 * experts)
    slot_count = experts * capacity
    route_count = token_count * routes_per
    flat_ids = expert_ids.reshape(-1)
    one_hot = flat_ids[:, None] == jnp.arange(experts, dtype=jnp.int32)[None, :]
    order = jnp.arange(route_count, dtype=jnp.int32)
    earlier = (order[None, :] < order[:, None]).astype(jnp.bfloat16)
    before = jnp.dot(earlier, one_hot.astype(jnp.bfloat16), preferred_element_type=jnp.float32)
    slot_rank = jnp.sum(jnp.where(one_hot, before, 0.0), axis=1).astype(jnp.int32)
    slot_of = (flat_ids * capacity + slot_rank).reshape(token_count, routes_per)
    slots = jnp.arange(slot_count, dtype=jnp.int32)
    token_pick = jnp.zeros((slot_count, token_count), jnp.bool_)
    slot_gate = jnp.zeros((slot_count,), jnp.float32)
    mix = jnp.zeros((token_count, slot_count), jnp.float32)
    spread = jnp.zeros((token_count, slot_count), jnp.bool_)
    for route in range(routes_per):
        chosen = slots[:, None] == slot_of[None, :, route]
        token_pick = token_pick | chosen
        slot_gate = slot_gate + jnp.sum(jnp.where(chosen, gate_values[None, :, route], 0.0), axis=1)
        chosen = slot_of[:, route, None] == slots[None, :]
        spread = spread | chosen
        mix = mix + jnp.where(chosen, gate_values[:, route, None], 0.0)
    token_pick = token_pick.astype(jnp.bfloat16)
    spread = spread.astype(jnp.bfloat16)
    mix_high = mix.astype(jnp.bfloat16)
    mix_low = (mix - mix_high.astype(jnp.float32)).astype(jnp.bfloat16)
    shaped = (experts, capacity, feature)

    def exchange(rows):
        return lax.all_to_all(
            rows.reshape(shaped), "expert", split_axis=0, concat_axis=0, tiled=True
        ).reshape(slot_count, feature)

    send_rows = jnp.dot(token_pick, tokens, preferred_element_type=jnp.float32).astype(jnp.bfloat16)
    slot_rows = exchange(send_rows)
    send_grads = (
        slot_gate[:, None] * jnp.dot(token_pick, cotangent, preferred_element_type=jnp.float32)
    ).astype(jnp.bfloat16)
    slot_grads = exchange(send_grads)
    shards = lax.axis_size("dp")

    def from_peer(block, flip):
        return lax.ppermute(block, "dp", [(rank, rank ^ flip) for rank in range(shards)])

    def gather(block):
        far = from_peer(block, 2)
        pair = jnp.concatenate([block, far], axis=0)
        return jnp.concatenate([pair, from_peer(pair, 1)], axis=0)

    def scatter(partial):
        partial = partial.astype(jnp.bfloat16)
        half = partial.shape[0] // 2
        near = from_peer(partial[half:], 1)
        pair = partial[:half].astype(jnp.float32) + near.astype(jnp.float32)
        far = from_peer(pair[half // 2 :].astype(jnp.bfloat16), 2)
        return (pair[: half // 2] + far.astype(jnp.float32)).astype(jnp.bfloat16)

    full_gate, full_up, full_down = gather(w_gate[0].T), gather(w_up[0].T), gather(w_down[0])
    gate_pre = contract_cols(slot_rows, full_gate)
    up_pre = contract_cols(slot_rows, full_up)
    activated, act_slope = swiglu_parts(gate_pre)
    hidden = (activated * up_pre).astype(jnp.bfloat16)
    out_rows = jnp.dot(hidden, full_down, preferred_element_type=jnp.float32).astype(jnp.bfloat16)
    out_rows, slot_grads = lax.optimization_barrier((out_rows, slot_grads))
    back_out = exchange(out_rows)
    grad_hidden = contract_cols(slot_grads, full_down)
    grad_gate_pre = (grad_hidden * up_pre * act_slope).astype(jnp.bfloat16)
    grad_up_pre = (grad_hidden * activated).astype(jnp.bfloat16)
    grad_rows = (
        jnp.dot(grad_gate_pre, full_gate, preferred_element_type=jnp.float32)
        + jnp.dot(grad_up_pre, full_up, preferred_element_type=jnp.float32)
    ).astype(jnp.bfloat16)
    grad_rows, back_out = lax.optimization_barrier((grad_rows, back_out))
    back_grad = exchange(grad_rows)
    grad_down = scatter(contract_rows(hidden, slot_grads))[None]
    grad_gate = scatter(contract_rows(grad_gate_pre, slot_rows)).T[None]
    grad_up = scatter(contract_rows(grad_up_pre, slot_rows)).T[None]
    mixed = (
        jnp.dot(mix_high, back_out, preferred_element_type=jnp.float32)
        + jnp.dot(mix_low, back_out, preferred_element_type=jnp.float32)
    ).astype(jnp.bfloat16)
    grad_tokens = jnp.dot(spread, back_grad, preferred_element_type=jnp.float32).astype(
        jnp.bfloat16
    )
    return (mixed, grad_tokens, grad_gate, grad_up, grad_down)


def solution(mesh):
    in_specs = (
        P(("dp", "expert"), None),
        P(("dp", "expert"), None),
        P(("dp", "expert"), None),
        P(("dp", "expert"), None),
        P("expert", None, "dp"),
        P("expert", None, "dp"),
        P("expert", "dp", None),
    )
    out_specs = (
        P(("dp", "expert"), None),
        P(("dp", "expert"), None),
        P("expert", None, "dp"),
        P("expert", None, "dp"),
        P("expert", "dp", None),
    )
    return jax.shard_map(body, mesh=mesh, in_specs=in_specs, out_specs=out_specs, check_vma=False)
```

```python
import jax
import jax.numpy as jnp
from jax import lax
from jax.sharding import PartitionSpec as P


def swiglu_parts(gate_pre):
    sigmoid_g = jax.nn.sigmoid(gate_pre)
    return (gate_pre * sigmoid_g, sigmoid_g * (1.0 + gate_pre * (1.0 - sigmoid_g)))


def contract_rows(left, right):
    return lax.dot_general(
        left, right, (((0,), (0,)), ((), ())), preferred_element_type=jnp.float32
    )


def contract_cols(left, right):
    return lax.dot_general(
        left, right, (((1,), (1,)), ((), ())), preferred_element_type=jnp.float32
    )


def body(tokens, expert_ids, gate_values, cotangent, w_gate, w_up, w_down):
    token_count, feature = tokens.shape
    routes_per = expert_ids.shape[1]
    experts = lax.axis_size("expert")
    capacity = 3 * token_count * routes_per // (2 * experts)
    slot_count = experts * capacity
    half = experts // 2
    opposite = [(rank, (rank + half) % experts) for rank in range(experts)]
    members = [[part * half + rank for rank in range(half)] for part in range(2)]

    def swap(block):
        return lax.ppermute(block, "expert", opposite)

    def with_far(block):
        return jnp.concatenate([block, swap(block)], axis=0)

    expert_ids, gate_values = with_far(expert_ids), with_far(gate_values)
    tokens, cotangent = with_far(tokens), with_far(cotangent)
    own_count, token_count, capacity = token_count, 2 * token_count, 2 * capacity
    route_count = token_count * routes_per
    flat_ids = expert_ids.reshape(-1) - lax.axis_index("expert") // half * half
    one_hot = flat_ids[:, None] == jnp.arange(half, dtype=jnp.int32)[None, :]
    order = jnp.arange(route_count, dtype=jnp.int32)
    earlier = (order[None, :] < order[:, None]).astype(jnp.bfloat16)
    before = jnp.dot(earlier, one_hot.astype(jnp.bfloat16), preferred_element_type=jnp.float32)
    slot_rank = jnp.sum(jnp.where(one_hot, before, 0.0), axis=1).astype(jnp.int32)
    slot_of = jnp.where(
        (flat_ids >= 0) & (flat_ids < half), flat_ids * capacity + slot_rank, -1
    ).reshape(token_count, routes_per)
    slots = jnp.arange(slot_count, dtype=jnp.int32)
    token_pick = jnp.zeros((slot_count, token_count), jnp.bool_)
    slot_gate = jnp.zeros((slot_count,), jnp.float32)
    mix = jnp.zeros((token_count, slot_count), jnp.float32)
    spread = jnp.zeros((token_count, slot_count), jnp.bool_)
    for route in range(routes_per):
        chosen = slots[:, None] == slot_of[None, :, route]
        token_pick = token_pick | chosen
        slot_gate = slot_gate + jnp.sum(jnp.where(chosen, gate_values[None, :, route], 0.0), axis=1)
        chosen = slot_of[:, route, None] == slots[None, :]
        spread = spread | chosen
        mix = mix + jnp.where(chosen, gate_values[:, route, None], 0.0)
    token_pick = token_pick.astype(jnp.bfloat16)
    spread = spread.astype(jnp.bfloat16)
    mix_high = mix.astype(jnp.bfloat16)
    mix_low = (mix - mix_high.astype(jnp.float32)).astype(jnp.bfloat16)
    shaped = (half, capacity, feature)

    def exchange(rows):
        return lax.all_to_all(
            rows.reshape(shaped),
            "expert",
            split_axis=0,
            concat_axis=0,
            tiled=True,
            axis_index_groups=members,
        ).reshape(slot_count, feature)

    send_rows = jnp.dot(token_pick, tokens, preferred_element_type=jnp.float32).astype(jnp.bfloat16)
    slot_rows = exchange(send_rows)
    send_grads = (
        slot_gate[:, None] * jnp.dot(token_pick, cotangent, preferred_element_type=jnp.float32)
    ).astype(jnp.bfloat16)
    slot_grads = exchange(send_grads)
    shards = lax.axis_size("dp")

    def from_peer(block, flip):
        return lax.ppermute(block, "dp", [(rank, rank ^ flip) for rank in range(shards)])

    def gather(block):
        far = from_peer(block, 2)
        pair = jnp.concatenate([block, far], axis=0)
        return jnp.concatenate([pair, from_peer(pair, 1)], axis=0)

    def scatter(partial):
        partial = partial.astype(jnp.bfloat16)
        half = partial.shape[0] // 2
        near = from_peer(partial[half:], 1)
        pair = partial[:half].astype(jnp.float32) + near.astype(jnp.float32)
        far = from_peer(pair[half // 2 :].astype(jnp.bfloat16), 2)
        return pair[: half // 2], far

    full_gate, full_up, full_down = gather(w_gate[0].T), gather(w_up[0].T), gather(w_down[0])
    gate_pre = contract_cols(slot_rows, full_gate)
    up_pre = contract_cols(slot_rows, full_up)
    activated, act_slope = swiglu_parts(gate_pre)
    hidden = (activated * up_pre).astype(jnp.bfloat16)
    out_rows = jnp.dot(hidden, full_down, preferred_element_type=jnp.float32).astype(jnp.bfloat16)
    out_rows, slot_grads = lax.optimization_barrier((out_rows, slot_grads))
    back_out = exchange(out_rows)
    grad_hidden = contract_cols(slot_grads, full_down)
    grad_gate_pre = (grad_hidden * up_pre * act_slope).astype(jnp.bfloat16)
    grad_up_pre = (grad_hidden * activated).astype(jnp.bfloat16)
    grad_rows = (
        jnp.dot(grad_gate_pre, full_gate, preferred_element_type=jnp.float32)
        + jnp.dot(grad_up_pre, full_up, preferred_element_type=jnp.float32)
    ).astype(jnp.bfloat16)
    grad_rows, back_out = lax.optimization_barrier((grad_rows, back_out))
    back_grad = exchange(grad_rows)
    sums = [
        scatter(contract_rows(hidden, slot_grads)),
        scatter(contract_rows(grad_gate_pre, slot_rows)),
        scatter(contract_rows(grad_up_pre, slot_rows)),
    ]

    def combine(weights, rows):
        own, far = (
            sum(jnp.dot(weight[part], rows, preferred_element_type=jnp.float32) for weight in weights)
            for part in (slice(0, own_count), slice(own_count, token_count))
        )
        return own, swap(far.astype(jnp.bfloat16))

    def total(own, far):
        return (own + far.astype(jnp.float32)).astype(jnp.bfloat16)

    own_mixed, far_mixed = combine((mix_high, mix_low), back_out)
    arrived, far_mixed = lax.optimization_barrier(([far for _, far in sums], far_mixed))
    mixed = total(own_mixed, far_mixed)
    grad_tokens = total(*combine((spread,), back_grad))
    grad_down, grad_gate, grad_up = (total(own, far) for (own, _), far in zip(sums, arrived))
    grad_down, grad_gate, grad_up = grad_down[None], grad_gate.T[None], grad_up.T[None]
    return (mixed, grad_tokens, grad_gate, grad_up, grad_down)


def solution(mesh):
    in_specs = (
        P(("dp", "expert"), None),
        P(("dp", "expert"), None),
        P(("dp", "expert"), None),
        P(("dp", "expert"), None),
        P("expert", None, "dp"),
        P("expert", None, "dp"),
        P("expert", "dp", None),
    )
    out_specs = (
        P(("dp", "expert"), None),
        P(("dp", "expert"), None),
        P("expert", None, "dp"),
        P("expert", None, "dp"),
        P("expert", "dp", None),
    )
    return jax.shard_map(body, mesh=mesh, in_specs=in_specs, out_specs=out_specs, check_vma=False)
```

```python
import jax
import jax.numpy as jnp
from jax import lax
from jax.sharding import PartitionSpec as P


def swiglu_parts(gate_pre):
    sigmoid_g = jax.nn.sigmoid(gate_pre)
    return (gate_pre * sigmoid_g, sigmoid_g * (1.0 + gate_pre * (1.0 - sigmoid_g)))


def contract_rows(left, right):
    return lax.dot_general(
        left, right, (((0,), (0,)), ((), ())), preferred_element_type=jnp.float32
    )


def contract_cols(left, right):
    return lax.dot_general(
        left, right, (((1,), (1,)), ((), ())), preferred_element_type=jnp.float32
    )


def body(tokens, expert_ids, gate_values, cotangent, w_gate, w_up, w_down):
    token_count, feature = tokens.shape
    routes_per = expert_ids.shape[1]
    experts = lax.axis_size("expert")
    capacity = 3 * token_count * routes_per // (2 * experts)
    slot_count = experts * capacity
    half = experts // 2
    opposite = [(rank, (rank + half) % experts) for rank in range(experts)]
    members = [[part * half + rank for rank in range(half)] for part in range(2)]

    def swap(block):
        return lax.ppermute(block, "expert", opposite)

    def with_far(block):
        return jnp.concatenate([block, swap(block)], axis=0)

    shards = lax.axis_size("dp")

    def from_peer(block, flip):
        return lax.ppermute(block, "dp", [(rank, rank ^ flip) for rank in range(shards)])

    expert_ids, gate_values = with_far(expert_ids), with_far(gate_values)
    gate_block = w_gate[0].T
    far_tokens, far_gate = lax.optimization_barrier((swap(tokens), from_peer(gate_block, 2)))
    tokens, cotangent = jnp.concatenate([tokens, far_tokens], axis=0), with_far(cotangent)
    own_count, token_count, capacity = token_count, 2 * token_count, 2 * capacity
    route_count = token_count * routes_per
    flat_ids = expert_ids.reshape(-1) - lax.axis_index("expert") // half * half
    one_hot = flat_ids[:, None] == jnp.arange(half, dtype=jnp.int32)[None, :]
    order = jnp.arange(route_count, dtype=jnp.int32)
    earlier = (order[None, :] < order[:, None]).astype(jnp.bfloat16)
    before = jnp.dot(earlier, one_hot.astype(jnp.bfloat16), preferred_element_type=jnp.float32)
    slot_rank = jnp.sum(jnp.where(one_hot, before, 0.0), axis=1).astype(jnp.int32)
    slot_of = jnp.where(
        (flat_ids >= 0) & (flat_ids < half), flat_ids * capacity + slot_rank, -1
    ).reshape(token_count, routes_per)
    slots = jnp.arange(slot_count, dtype=jnp.int32)
    token_pick = jnp.zeros((slot_count, token_count), jnp.bool_)
    slot_gate = jnp.zeros((slot_count,), jnp.float32)
    mix = jnp.zeros((token_count, slot_count), jnp.float32)
    spread = jnp.zeros((token_count, slot_count), jnp.bool_)
    for route in range(routes_per):
        chosen = slots[:, None] == slot_of[None, :, route]
        token_pick = token_pick | chosen
        slot_gate = slot_gate + jnp.sum(jnp.where(chosen, gate_values[None, :, route], 0.0), axis=1)
        chosen = slot_of[:, route, None] == slots[None, :]
        spread = spread | chosen
        mix = mix + jnp.where(chosen, gate_values[:, route, None], 0.0)
    token_pick = token_pick.astype(jnp.bfloat16)
    spread = spread.astype(jnp.bfloat16)
    mix_high = mix.astype(jnp.bfloat16)
    mix_low = (mix - mix_high.astype(jnp.float32)).astype(jnp.bfloat16)
    shaped = (half, capacity, feature)

    def exchange(rows):
        return lax.all_to_all(
            rows.reshape(shaped),
            "expert",
            split_axis=0,
            concat_axis=0,
            tiled=True,
            axis_index_groups=members,
        ).reshape(slot_count, feature)

    send_rows = jnp.dot(token_pick, tokens, preferred_element_type=jnp.float32).astype(jnp.bfloat16)
    slot_rows = exchange(send_rows)
    send_grads = (
        slot_gate[:, None] * jnp.dot(token_pick, cotangent, preferred_element_type=jnp.float32)
    ).astype(jnp.bfloat16)
    slot_grads = exchange(send_grads)
    def gather(block, far=None):
        far = from_peer(block, 2) if far is None else far
        pair = jnp.concatenate([block, far], axis=0)
        return jnp.concatenate([pair, from_peer(pair, 1)], axis=0)

    def scatter(partial):
        partial = partial.astype(jnp.bfloat16)
        half = partial.shape[0] // 2
        near = from_peer(partial[half:], 1)
        pair = partial[:half].astype(jnp.float32) + near.astype(jnp.float32)
        far = from_peer(pair[half // 2 :].astype(jnp.bfloat16), 2)
        return pair[: half // 2], far

    full_gate, full_up, full_down = gather(gate_block, far_gate), gather(w_up[0].T), gather(w_down[0])
    gate_pre = contract_cols(slot_rows, full_gate)
    up_pre = contract_cols(slot_rows, full_up)
    activated, act_slope = swiglu_parts(gate_pre)
    hidden = (activated * up_pre).astype(jnp.bfloat16)
    out_rows = jnp.dot(hidden, full_down, preferred_element_type=jnp.float32).astype(jnp.bfloat16)
    out_rows, slot_grads = lax.optimization_barrier((out_rows, slot_grads))
    back_out = exchange(out_rows)
    grad_hidden = contract_cols(slot_grads, full_down)
    grad_gate_pre = (grad_hidden * up_pre * act_slope).astype(jnp.bfloat16)
    grad_up_pre = (grad_hidden * activated).astype(jnp.bfloat16)
    grad_rows = (
        jnp.dot(grad_gate_pre, full_gate, preferred_element_type=jnp.float32)
        + jnp.dot(grad_up_pre, full_up, preferred_element_type=jnp.float32)
    ).astype(jnp.bfloat16)
    grad_rows, back_out = lax.optimization_barrier((grad_rows, back_out))
    back_grad = exchange(grad_rows)
    sums = [
        scatter(contract_rows(hidden, slot_grads)),
        scatter(contract_rows(grad_gate_pre, slot_rows)),
        scatter(contract_rows(grad_up_pre, slot_rows)),
    ]

    def combine(weights, rows):
        own, far = (
            sum(jnp.dot(weight[part], rows, preferred_element_type=jnp.float32) for weight in weights)
            for part in (slice(0, own_count), slice(own_count, token_count))
        )
        return own, swap(far.astype(jnp.bfloat16))

    def total(own, far):
        return (own + far.astype(jnp.float32)).astype(jnp.bfloat16)

    own_mixed, far_mixed = combine((mix_high, mix_low), back_out)
    own_grad, far_grad = combine((spread,), back_grad)
    arrived, far_mixed, far_grad = lax.optimization_barrier(
        ([far for _, far in sums], far_mixed, far_grad)
    )
    mixed, grad_tokens = total(own_mixed, far_mixed), total(own_grad, far_grad)
    grad_down, grad_gate, grad_up = (total(own, far) for (own, _), far in zip(sums, arrived))
    grad_down, grad_gate, grad_up = grad_down[None], grad_gate.T[None], grad_up.T[None]
    return (mixed, grad_tokens, grad_gate, grad_up, grad_down)


def solution(mesh):
    in_specs = (
        P(("dp", "expert"), None),
        P(("dp", "expert"), None),
        P(("dp", "expert"), None),
        P(("dp", "expert"), None),
        P("expert", None, "dp"),
        P("expert", None, "dp"),
        P("expert", "dp", None),
    )
    out_specs = (
        P(("dp", "expert"), None),
        P(("dp", "expert"), None),
        P("expert", None, "dp"),
        P("expert", None, "dp"),
        P("expert", "dp", None),
    )
    return jax.shard_map(body, mesh=mesh, in_specs=in_specs, out_specs=out_specs, check_vma=False)
```

```python
import jax
import jax.numpy as jnp
from jax import lax
from jax.sharding import PartitionSpec as P


def swiglu_parts(gate_pre):
    sigmoid_g = jax.nn.sigmoid(gate_pre)
    return (gate_pre * sigmoid_g, sigmoid_g * (1.0 + gate_pre * (1.0 - sigmoid_g)))


def contract_rows(left, right):
    return lax.dot_general(
        left, right, (((0,), (0,)), ((), ())), preferred_element_type=jnp.float32
    )


def contract_cols(left, right):
    return lax.dot_general(
        left, right, (((1,), (1,)), ((), ())), preferred_element_type=jnp.float32
    )


def body(tokens, expert_ids, gate_values, cotangent, w_gate, w_up, w_down):
    token_count, feature = tokens.shape
    routes_per = expert_ids.shape[1]
    experts = lax.axis_size("expert")
    capacity = 3 * token_count * routes_per // (2 * experts)
    slot_count = experts * capacity
    route_count = token_count * routes_per
    flat_ids = expert_ids.reshape(-1)
    one_hot = flat_ids[:, None] == jnp.arange(experts, dtype=jnp.int32)[None, :]
    order = jnp.arange(route_count, dtype=jnp.int32)
    earlier = (order[None, :] < order[:, None]).astype(jnp.bfloat16)
    before = jnp.dot(earlier, one_hot.astype(jnp.bfloat16), preferred_element_type=jnp.float32)
    slot_rank = jnp.sum(jnp.where(one_hot, before, 0.0), axis=1).astype(jnp.int32)
    slot_of = (flat_ids * capacity + slot_rank).reshape(token_count, routes_per)
    slots = jnp.arange(slot_count, dtype=jnp.int32)
    token_pick = jnp.zeros((slot_count, token_count), jnp.bool_)
    slot_gate = jnp.zeros((slot_count,), jnp.float32)
    mix = jnp.zeros((token_count, slot_count), jnp.float32)
    spread = jnp.zeros((token_count, slot_count), jnp.bool_)
    for route in range(routes_per):
        chosen = slots[:, None] == slot_of[None, :, route]
        token_pick = token_pick | chosen
        slot_gate = slot_gate + jnp.sum(jnp.where(chosen, gate_values[None, :, route], 0.0), axis=1)
        chosen = slot_of[:, route, None] == slots[None, :]
        spread = spread | chosen
        mix = mix + jnp.where(chosen, gate_values[:, route, None], 0.0)
    token_pick = token_pick.astype(jnp.bfloat16)
    spread = spread.astype(jnp.bfloat16)
    mix_high = mix.astype(jnp.bfloat16)
    mix_low = (mix - mix_high.astype(jnp.float32)).astype(jnp.bfloat16)
    shaped = (experts, capacity, feature)

    def exchange(rows):
        return lax.all_to_all(
            rows.reshape(shaped), "expert", split_axis=0, concat_axis=0, tiled=True
        ).reshape(slot_count, feature)

    send_rows = jnp.dot(token_pick, tokens, preferred_element_type=jnp.float32).astype(jnp.bfloat16)
    slot_rows = exchange(send_rows)
    send_grads = (
        slot_gate[:, None] * jnp.dot(token_pick, cotangent, preferred_element_type=jnp.float32)
    ).astype(jnp.bfloat16)
    slot_grads = exchange(send_grads)
    shards = lax.axis_size("dp")

    def from_peer(block, flip):
        return lax.ppermute(block, "dp", [(rank, rank ^ flip) for rank in range(shards)])

    def gather(block):
        far = from_peer(block, 2)
        pair = jnp.concatenate([block, far], axis=0)
        return jnp.concatenate([pair, from_peer(pair, 1)], axis=0)

    def scatter(partial):
        partial = partial.astype(jnp.bfloat16)
        half = partial.shape[0] // 2
        near = from_peer(partial[half:], 1)
        pair = partial[:half].astype(jnp.float32) + near.astype(jnp.float32)
        far = from_peer(pair[half // 2 :].astype(jnp.bfloat16), 2)
        return pair[: half // 2], far

    def total(own, far):
        return (own + far.astype(jnp.float32)).astype(jnp.bfloat16)

    full_gate, full_up, full_down = gather(w_gate[0].T), gather(w_up[0].T), gather(w_down[0])
    gate_pre = contract_cols(slot_rows, full_gate)
    up_pre = contract_cols(slot_rows, full_up)
    activated, act_slope = swiglu_parts(gate_pre)
    hidden = (activated * up_pre).astype(jnp.bfloat16)
    out_rows = jnp.dot(hidden, full_down, preferred_element_type=jnp.float32).astype(jnp.bfloat16)
    out_rows, slot_grads = lax.optimization_barrier((out_rows, slot_grads))
    back_out = exchange(out_rows)
    grad_hidden = contract_cols(slot_grads, full_down)
    grad_gate_pre = (grad_hidden * up_pre * act_slope).astype(jnp.bfloat16)
    grad_up_pre = (grad_hidden * activated).astype(jnp.bfloat16)
    grad_rows = (
        jnp.dot(grad_gate_pre, full_gate, preferred_element_type=jnp.float32)
        + jnp.dot(grad_up_pre, full_up, preferred_element_type=jnp.float32)
    ).astype(jnp.bfloat16)
    grad_rows, back_out = lax.optimization_barrier((grad_rows, back_out))
    back_grad = exchange(grad_rows)
    own_down, far_down = scatter(contract_rows(hidden, slot_grads))
    grad_gate = total(*scatter(contract_rows(grad_gate_pre, slot_rows))).T[None]
    grad_up = total(*scatter(contract_rows(grad_up_pre, slot_rows))).T[None]
    mixed = (
        jnp.dot(mix_high, back_out, preferred_element_type=jnp.float32)
        + jnp.dot(mix_low, back_out, preferred_element_type=jnp.float32)
    ).astype(jnp.bfloat16)
    grad_tokens = jnp.dot(spread, back_grad, preferred_element_type=jnp.float32).astype(
        jnp.bfloat16
    )
    far_down, mixed, grad_tokens = lax.optimization_barrier((far_down, mixed, grad_tokens))
    grad_down = total(own_down, far_down)[None]
    return (mixed, grad_tokens, grad_gate, grad_up, grad_down)


def solution(mesh):
    in_specs = (
        P(("dp", "expert"), None),
        P(("dp", "expert"), None),
        P(("dp", "expert"), None),
        P(("dp", "expert"), None),
        P("expert", None, "dp"),
        P("expert", None, "dp"),
        P("expert", "dp", None),
    )
    out_specs = (
        P(("dp", "expert"), None),
        P(("dp", "expert"), None),
        P("expert", None, "dp"),
        P("expert", None, "dp"),
        P("expert", "dp", None),
    )
    return jax.shard_map(body, mesh=mesh, in_specs=in_specs, out_specs=out_specs, check_vma=False)
```

```python
import jax
import jax.numpy as jnp
from jax import lax
from jax.sharding import PartitionSpec as P


def swiglu_parts(gate_pre):
    sigmoid_g = jax.nn.sigmoid(gate_pre)
    return (gate_pre * sigmoid_g, sigmoid_g * (1.0 + gate_pre * (1.0 - sigmoid_g)))


def contract_rows(left, right):
    return lax.dot_general(
        left, right, (((0,), (0,)), ((), ())), preferred_element_type=jnp.float32
    )


def contract_cols(left, right):
    return lax.dot_general(
        left, right, (((1,), (1,)), ((), ())), preferred_element_type=jnp.float32
    )


def body(tokens, expert_ids, gate_values, cotangent, w_gate, w_up, w_down):
    token_count, feature = tokens.shape
    routes_per = expert_ids.shape[1]
    experts = lax.axis_size("expert")
    capacity = 3 * token_count * routes_per // (2 * experts)
    slot_count = experts * capacity
    route_count = token_count * routes_per
    flat_ids = expert_ids.reshape(-1)
    one_hot = flat_ids[:, None] == jnp.arange(experts, dtype=jnp.int32)[None, :]
    order = jnp.arange(route_count, dtype=jnp.int32)
    earlier = (order[None, :] < order[:, None]).astype(jnp.bfloat16)
    before = jnp.dot(earlier, one_hot.astype(jnp.bfloat16), preferred_element_type=jnp.float32)
    slot_rank = jnp.sum(jnp.where(one_hot, before, 0.0), axis=1).astype(jnp.int32)
    slot_of = (flat_ids * capacity + slot_rank).reshape(token_count, routes_per)
    slots = jnp.arange(slot_count, dtype=jnp.int32)
    token_pick = jnp.zeros((slot_count, token_count), jnp.bool_)
    slot_gate = jnp.zeros((slot_count,), jnp.float32)
    mix = jnp.zeros((token_count, slot_count), jnp.float32)
    spread = jnp.zeros((token_count, slot_count), jnp.bool_)
    for route in range(routes_per):
        chosen = slots[:, None] == slot_of[None, :, route]
        token_pick = token_pick | chosen
        slot_gate = slot_gate + jnp.sum(jnp.where(chosen, gate_values[None, :, route], 0.0), axis=1)
        chosen = slot_of[:, route, None] == slots[None, :]
        spread = spread | chosen
        mix = mix + jnp.where(chosen, gate_values[:, route, None], 0.0)
    token_pick = token_pick.astype(jnp.bfloat16)
    spread = spread.astype(jnp.bfloat16)
    mix_high = mix.astype(jnp.bfloat16)
    mix_low = (mix - mix_high.astype(jnp.float32)).astype(jnp.bfloat16)
    shaped = (experts, capacity, feature)

    def exchange(rows):
        return lax.all_to_all(
            rows.reshape(shaped), "expert", split_axis=0, concat_axis=0, tiled=True
        ).reshape(slot_count, feature)

    send_rows = jnp.dot(token_pick, tokens, preferred_element_type=jnp.float32).astype(jnp.bfloat16)
    slot_rows = exchange(send_rows)
    send_grads = (
        slot_gate[:, None] * jnp.dot(token_pick, cotangent, preferred_element_type=jnp.float32)
    ).astype(jnp.bfloat16)
    slot_grads = exchange(send_grads)
    shards = lax.axis_size("dp")

    def from_peer(block, flip):
        return lax.ppermute(block, "dp", [(rank, rank ^ flip) for rank in range(shards)])

    def gather(block):
        far = from_peer(block, 2)
        pair = jnp.concatenate([block, far], axis=0)
        return jnp.concatenate([pair, from_peer(pair, 1)], axis=0)

    def scatter(left, right):
        half = left.shape[1] // 2
        near = from_peer(contract_rows(left[:, half:], right).astype(jnp.bfloat16), 1)
        pair = contract_rows(left[:, :half], right) + near.astype(jnp.float32)
        far = from_peer(pair[half // 2 :].astype(jnp.bfloat16), 2)
        return (pair[: half // 2] + far.astype(jnp.float32)).astype(jnp.bfloat16)

    full_gate, full_up, full_down = gather(w_gate[0].T), gather(w_up[0].T), gather(w_down[0])
    gate_pre = contract_cols(slot_rows, full_gate)
    up_pre = contract_cols(slot_rows, full_up)
    activated, act_slope = swiglu_parts(gate_pre)
    hidden = (activated * up_pre).astype(jnp.bfloat16)
    out_rows = jnp.dot(hidden, full_down, preferred_element_type=jnp.float32).astype(jnp.bfloat16)
    out_rows, slot_grads = lax.optimization_barrier((out_rows, slot_grads))
    back_out = exchange(out_rows)
    grad_hidden = contract_cols(slot_grads, full_down)
    grad_gate_pre = (grad_hidden * up_pre * act_slope).astype(jnp.bfloat16)
    grad_up_pre = (grad_hidden * activated).astype(jnp.bfloat16)
    grad_rows = (
        jnp.dot(grad_gate_pre, full_gate, preferred_element_type=jnp.float32)
        + jnp.dot(grad_up_pre, full_up, preferred_element_type=jnp.float32)
    ).astype(jnp.bfloat16)
    grad_rows, back_out = lax.optimization_barrier((grad_rows, back_out))
    back_grad = exchange(grad_rows)
    grad_down = scatter(hidden, slot_grads)[None]
    grad_gate = scatter(grad_gate_pre, slot_rows).T[None]
    grad_up = scatter(grad_up_pre, slot_rows).T[None]
    mixed = (
        jnp.dot(mix_high, back_out, preferred_element_type=jnp.float32)
        + jnp.dot(mix_low, back_out, preferred_element_type=jnp.float32)
    ).astype(jnp.bfloat16)
    grad_tokens = jnp.dot(spread, back_grad, preferred_element_type=jnp.float32).astype(
        jnp.bfloat16
    )
    return (mixed, grad_tokens, grad_gate, grad_up, grad_down)


def solution(mesh):
    in_specs = (
        P(("dp", "expert"), None),
        P(("dp", "expert"), None),
        P(("dp", "expert"), None),
        P(("dp", "expert"), None),
        P("expert", None, "dp"),
        P("expert", None, "dp"),
        P("expert", "dp", None),
    )
    out_specs = (
        P(("dp", "expert"), None),
        P(("dp", "expert"), None),
        P("expert", None, "dp"),
        P("expert", None, "dp"),
        P("expert", "dp", None),
    )
    return jax.shard_map(body, mesh=mesh, in_specs=in_specs, out_specs=out_specs, check_vma=False)
```
